32 devices in a mesh: dp: 8 (over y, x, core), tensor: 4 (over z).
Axes of the slice: x: 2, y: 2, z: 4, core: 2. Of those that a mesh axis runs over, the one named last changes fastest.
Arguments:
- inputs: float32 [1024, 2048], P(('dp', 'tensor')), parts along dimension 0, may hold values from -6 to 6
- out_grad: float32 [1024, 2048], P(('dp', 'tensor')), parts along dimension 0, may hold values from -6 to 6
- pre_saved: bfloat16 [1024, 1536], P('dp', 'tensor'), parts along dimension 0, may hold values from -6 to 6
- w_in: bfloat16 [2048, 1536], P(None, 'tensor'), may hold values from -0.125 to 0.125
- w_out_t: bfloat16 [2048, 1536], P(None, 'tensor'), may hold values from -0.15625 to 0.15625
Outputs:
- input_grad: float32 [1024, 2048], P(('dp', 'tensor')), parts along dimension 0
- grad_w_in: bfloat16 [16384, 1536], P('dp', 'tensor'), parts along dimension 0
- grad_w_out_t: bfloat16 [16384, 1536], P('dp', 'tensor'), parts along dimension 0
The draws below stay inside these ranges and needn't reach their ends.
There are 8 independent parts, one for each index of `dp`. The reference program is written for one: setup_inputs(seed, part) draws one part's arguments, and reference() takes and returns one part's arrays. A program takes and returns all parts, laid end to end along the dimension named above; an argument that names none is the same for every part. Nothing has to cross between parts.
All inputs are finite; a program needn't handle non-finite values.
Results may differ from the reference program's by a relative error of at most 0.02.
Values may be sent and summed in bfloat16 or wider, within the bound.
No kernel may reach another device: no remote copies, remote signals or barrier semaphores. Data moves between devices by JAX's collectives and lax.ppermute only.
A program may use at most 64 MiB of HBM per device.

```python
import jax
import jax.numpy as jnp
from jax import lax

D = 2048
FF_DEV = 384
FF = 1536
ROWS = 128
N_TENSOR = 4


def block_scale(own_key, dims, pieces, least, high):
    level = 1.0
    for axis_at, parts in pieces:
        draws = jax.random.uniform(jax.random.fold_in(jax.random.fold_in(own_key, 6), axis_at), (parts,), jnp.float32, least / len(pieces), high / len(pieces))
        level = level * jnp.repeat(jnp.exp(draws), dims[axis_at] // parts).reshape((-1,) + (1,) * (len(dims) - 1 - axis_at))
    return level


def normal_values(key, extent, width, reach, split=(), dtype=jnp.bfloat16):
    result = width * jax.random.normal(key, extent, jnp.float32)
    if split:
        result = result * block_scale(key, extent, split, -0.22, 0.18)
    return jnp.clip(result, -reach, reach).astype(dtype)


def setup_inputs(seed: int = 0, part: int = 0) -> dict:
    keys = jax.random.split(jax.random.key(seed), 6)
    part_splits = jax.random.split(jax.random.fold_in(keys[5], part), 6)
    inputs = normal_values(part_splits[0], (ROWS, D), 1.0, 6.0, ((0, 4),), jnp.float32)
    out_grad = normal_values(part_splits[1], (ROWS, D), 1.0, 6.0, ((0, 4),), jnp.float32)
    pre_saved = normal_values(part_splits[2], (ROWS, FF), 1.0, 6.0, ((1, 4),))
    w_in = normal_values(keys[3], (D, FF), D ** -0.5, 0.125, ((1, 4),))
    w_out_t = normal_values(keys[4], (D, FF), FF ** -0.5, 0.15625, ((1, 4),))
    return dict(inputs=inputs, out_grad=out_grad, pre_saved=pre_saved, w_in=w_in, w_out_t=w_out_t)


def contract_rows(left, right):
    return lax.dot_general(left, right, (((0,), (0,)), ((), ())), preferred_element_type=jnp.float32)


def contract_cols(left, right):
    return lax.dot_general(left, right, (((1,), (1,)), ((), ())), preferred_element_type=jnp.float32)


def reference(inputs, out_grad, pre_saved, w_in, w_out_t):
    inputs_bf = inputs.astype(jnp.bfloat16)
    grad_bf = out_grad.astype(jnp.bfloat16)
    activ = jnp.maximum(pre_saved, jnp.zeros_like(pre_saved))
    grad_w_out_t = contract_rows(grad_bf, activ).astype(jnp.bfloat16)
    back = jnp.dot(grad_bf, w_out_t, preferred_element_type=jnp.float32)
    hid_grad = jnp.where(pre_saved > 0.0, back, 0.0).astype(jnp.bfloat16)
    grad_w_in = contract_rows(inputs_bf, hid_grad).astype(jnp.bfloat16)
    hid_blocks = hid_grad.reshape(hid_grad.shape[0], N_TENSOR, FF_DEV).transpose(1, 0, 2)
    weight_blocks = w_in.reshape(w_in.shape[0], N_TENSOR, FF_DEV).transpose(1, 0, 2)

    def add_block(total, pair):
        partial_value = contract_cols(pair[0], pair[1]).astype(jnp.bfloat16)
        partial_value = lax.optimization_barrier(partial_value)
        return total + partial_value.astype(jnp.float32), None

    start = jnp.zeros((hid_grad.shape[0], w_in.shape[0]), jnp.float32)
    input_grad, unused = lax.scan(add_block, start, (hid_blocks, weight_blocks))
    return input_grad, grad_w_in, grad_w_out_t
```

```python
import functools

import jax
import jax.numpy as jnp
from jax import lax
from jax.experimental import pallas as pl
from jax.experimental.pallas import tpu as pltpu
from jax.sharding import PartitionSpec as P

AXIS = "tensor"
HBM = pl.BlockSpec(memory_space=pl.ANY)
VMEM = pl.BlockSpec(memory_space=pltpu.VMEM)
SMEM = pl.BlockSpec(memory_space=pltpu.SMEM)
PARAMS = pltpu.CompilerParams(vmem_limit_bytes=32 * 1024 * 1024)


def largest_tile(extent, limit):
    tile = min(extent, limit)
    while extent % tile:
        tile //= 2
    return tile


def cost(flops, moved):
    return pl.CostEstimate(flops=flops, bytes_accessed=moved, transcendentals=0)


def team_of(n):
    return 2 if n % 2 == 0 else 1


def owner(me, slot, n):
    team = team_of(n)
    ahead = lax.rem(me + slot // team * team, n)
    if slot % team == 0:
        return ahead
    return ahead + 1 - 2 * lax.rem(ahead, 2)


def pre_block(ref, me, slot, n, rows):
    return ref[pl.ds(pl.multiple_of(owner(me, slot, n) * rows, rows), rows), :]


def stack(refs, starts, rows, columns=slice(None)):
    return jnp.concatenate([ref[s : s + rows, columns] for ref, s in zip(refs, starts)], axis=0)


def pair_kernel(upper_ref, lower_ref, both_ref):
    rows = upper_ref.shape[0]
    both_ref[:rows, :] = upper_ref[...]
    both_ref[rows:, :] = lower_ref[...].astype(both_ref.dtype)


def pair(upper, lower):
    rows, width = upper.shape
    return pl.pallas_call(
        pair_kernel,
        out_shape=jax.ShapeDtypeStruct((2 * rows, width), upper.dtype),
        in_specs=[VMEM] * 2,
        out_specs=VMEM,
        cost_estimate=cost(0, 10 * rows * width),
        compiler_params=PARAMS,
        name="pair",
    )(upper, lower)


def share(pre, grads, w_out_ref, w_in_ref, emit):
    back = jnp.dot(grads, w_out_ref[...], preferred_element_type=jnp.float32)
    hid = jnp.where(pre.astype(jnp.float32) > 0.0, back, 0.0).astype(jnp.bfloat16)
    width = w_in_ref.shape[0]
    tile = largest_tile(width, 512)
    for start in range(0, width, tile):
        columns = slice(start, start + tile)
        part = lax.dot_general(
            hid,
            w_in_ref[columns, :],
            (((1,), (1,)), ((), ())),
            preferred_element_type=jnp.float32,
        )
        emit(columns, part)
    return hid


def own_kernel(n, me_ref, pre_ref, w_out_ref, w_in_ref, grad_ref, hid_ref, part_ref):
    rows = part_ref.shape[0]

    def emit(columns, part):
        part_ref[:, columns] = part

    pre = pre_block(pre_ref, me_ref[0], 0, n, rows)
    hid_ref[...] = share(pre, grad_ref[...], w_out_ref, w_in_ref, emit)


def own_block(n, me, pre, w_out_t, w_in, grad):
    hidden, width = pre.shape[1], w_in.shape[0]
    rows = pre.shape[0] // n
    return pl.pallas_call(
        functools.partial(own_kernel, n),
        out_shape=[
            jax.ShapeDtypeStruct((rows, hidden), jnp.bfloat16),
            jax.ShapeDtypeStruct((rows, width), jnp.float32),
        ],
        in_specs=[SMEM] + [VMEM] * 4,
        out_specs=[VMEM] * 2,
        cost_estimate=cost(4 * rows * width * hidden, 4 * width * hidden + 6 * rows * width),
        compiler_params=PARAMS,
        name="own_block",
    )(me, pre, w_out_t, w_in, grad)


def partial_kernel(n, starts, me_ref, pre_ref, w_out_ref, w_in_ref, *refs):
    grad_refs, hid_ref, part_refs = refs[: n - 1], refs[n - 1], refs[n:]
    rows = part_refs[0].shape[0]
    me = me_ref[0]

    def emit(columns, part):
        part = part.astype(jnp.bfloat16)
        for k, ref in enumerate(part_refs):
            ref[:, columns] = part[k * rows : (k + 1) * rows]

    pre = jnp.concatenate([pre_block(pre_ref, me, k, n, rows) for k in range(1, n)], axis=0)
    hid_ref[...] = share(pre, stack(grad_refs, starts, rows), w_out_ref, w_in_ref, emit)


def partials(n, me, pre, w_out_t, w_in, pieces):
    hidden, width = pre.shape[1], w_in.shape[0]
    count = n - 1
    rows = pre.shape[0] // n
    grads, starts = zip(*pieces)
    return pl.pallas_call(
        functools.partial(partial_kernel, n, starts),
        out_shape=[jax.ShapeDtypeStruct((count * rows, hidden), jnp.bfloat16)]
        + [jax.ShapeDtypeStruct((rows, width), jnp.bfloat16)] * count,
        in_specs=[SMEM] + [VMEM] * (count + 3),
        out_specs=[VMEM] * (count + 1),
        cost_estimate=cost(
            4 * count * rows * width * hidden,
            4 * count * rows * (width + hidden) + 4 * width * hidden,
        ),
        compiler_params=PARAMS,
        name="partials",
    )(me, pre, w_out_t, w_in, *grads)


def weight_tiles(lefts, starts, right, out_hbm, buffer, sems):
    rows = right.shape[0] // len(lefts)
    moves = []
    for k in range(sems.shape[0]):
        tile = buffer.shape[0] // sems.shape[0]
        columns = slice(k * tile, (k + 1) * tile)
        buffer[columns, :] = lax.dot_general(
            stack(lefts, starts, rows, columns),
            right,
            (((0,), (0,)), ((), ())),
            preferred_element_type=jnp.float32,
        ).astype(buffer.dtype)
        moves.append(pltpu.make_async_copy(buffer.at[columns], out_hbm.at[columns], sems.at[k]))
        moves[k].start()
    return moves


def out_kernel(n, starts, me_ref, pre_ref, *refs):
    left_refs, (out_hbm, buffer, sems) = refs[:n], refs[n:]
    me, rows = me_ref[0], pre_ref.shape[0] // n
    pre = jnp.concatenate([pre_block(pre_ref, me, k, n, rows) for k in range(n)], axis=0)
    activ = jnp.maximum(pre, jnp.zeros_like(pre))
    for move in weight_tiles(left_refs, starts, activ, out_hbm, buffer, sems):
        move.wait()


def in_kernel(n, starts, hid_count, *refs):
    left_refs, hid_refs, (out_hbm, buffer, sems) = refs[:n], refs[n : n + hid_count], refs[n + hid_count :]
    hid = jnp.concatenate([ref[...] for ref in hid_refs], axis=0)
    for move in weight_tiles(left_refs, starts, hid, out_hbm, buffer, sems):
        move.wait()


def weight_scratch(width, hidden):
    return [
        pltpu.VMEM((width, hidden), jnp.bfloat16),
        pltpu.SemaphoreType.DMA((width // largest_tile(width, 256),)),
    ]


def weight_cost(total, width, hidden):
    return cost(2 * total * width * hidden, 2 * total * (width + hidden) + 2 * width * hidden)


def out_weight_grad(n, me, pieces, pre):
    lefts, starts = zip(*pieces)
    width, hidden = lefts[0].shape[1], pre.shape[1]
    return pl.pallas_call(
        functools.partial(out_kernel, n, starts),
        out_shape=jax.ShapeDtypeStruct((width, hidden), jnp.bfloat16),
        in_specs=[SMEM] + [VMEM] * (n + 1),
        out_specs=HBM,
        scratch_shapes=weight_scratch(width, hidden),
        cost_estimate=weight_cost(pre.shape[0], width, hidden),
        compiler_params=PARAMS,
        name="out_weight_grad",
    )(me, pre, *lefts)


def in_weight_grad(n, pieces, hids):
    lefts, starts = zip(*pieces)
    width, hidden = lefts[0].shape[1], hids[0].shape[1]
    return pl.pallas_call(
        functools.partial(in_kernel, n, starts, len(hids)),
        out_shape=jax.ShapeDtypeStruct((width, hidden), jnp.bfloat16),
        in_specs=[VMEM] * (n + len(hids)),
        out_specs=HBM,
        scratch_shapes=weight_scratch(width, hidden),
        cost_estimate=weight_cost(sum(hid.shape[0] for hid in hids), width, hidden),
        compiler_params=PARAMS,
        name="in_weight_grad",
    )(*lefts, *hids)


def owner_of(me, slot, n):
    ahead = (me + slot // team_of(n) * team_of(n)) % n
    return ahead ^ (slot % team_of(n))


def from_slot(n, block, slot):
    return lax.ppermute(block, AXIS, [(owner_of(i, slot, n), i) for i in range(n)])


def to_slot(n, block, slot):
    return lax.ppermute(block, AXIS, [(i, owner_of(i, slot, n)) for i in range(n)])


def later(values, *things):
    return lax.optimization_barrier((values, things))[0]


def on_device(inputs, out_grad, pre_saved, w_in, w_out_t, *, n):
    team = team_of(n)
    far = range(team, n, team)
    rows = inputs.shape[0]
    me = lax.axis_index(AXIS).astype(jnp.int32).reshape(1)
    grad_bf = out_grad.astype(jnp.bfloat16)
    far_grads = [from_slot(n, grad_bf, k) for k in far]
    both = pair(grad_bf, inputs)
    grads, ins = {0: (grad_bf, 0)}, {}
    if team == 2:
        near = from_slot(n, both, 1)
        grads[1], ins[1] = (near, 0), (near, rows)
    own_hid, input_grad = own_block(n, me, pre_saved, w_out_t, w_in, grad_bf)
    hids = [own_hid]
    far_grads = later(far_grads, own_hid)
    for k, got in zip(far, far_grads):
        grads[k] = (got, 0)
        if team == 2:
            grads[k + 1] = (from_slot(n, got, 1), 0)
    inputs_bf = later(inputs, far_grads).astype(jnp.bfloat16)
    ins[0] = (inputs_bf, 0)
    far_ins = [from_slot(n, inputs_bf, k) for k in far]
    arrived, pre = [], pre_saved
    if n > 1:
        hid, *parts = partials(n, me, pre_saved, w_out_t, w_in, [grads[k] for k in range(1, n)])
        pre = later(pre, parts)
        parts = [None] + parts
        hids.append(hid)
        sums = [parts[k] + from_slot(n, parts[k + 1], 1) if team == 2 else parts[k] for k in far]
        sums, parts = lax.optimization_barrier((sums, parts))
        arrived = [to_slot(n, block, k) for k, block in zip(far, sums)]
        if team == 2:
            arrived.append(from_slot(n, parts[1], 1))
    grad_w_out_t = out_weight_grad(n, me, [grads[k] for k in range(n)], pre)
    far_ins = later(far_ins, grad_w_out_t)
    for k, got in zip(far, far_ins):
        ins[k] = (got, 0)
        if team == 2:
            ins[k + 1] = (from_slot(n, got, 1), 0)
    grad_w_in = in_weight_grad(n, [ins[k] for k in range(n)], hids)
    for block in arrived:
        input_grad = input_grad + block.astype(jnp.float32)
    return (input_grad, grad_w_in, grad_w_out_t)


def solution(mesh):
    in_specs = (
        P(("dp", AXIS), None),
        P(("dp", AXIS), None),
        P("dp", AXIS),
        P(None, AXIS),
        P(None, AXIS),
    )
    out_specs = (P(("dp", AXIS), None), P("dp", AXIS), P("dp", AXIS))
    return jax.shard_map(
        functools.partial(on_device, n=mesh.shape[AXIS]),
        mesh=mesh,
        in_specs=in_specs,
        out_specs=out_specs,
        check_vma=False,
    )
```

```python
import functools

import jax
import jax.numpy as jnp
from jax import lax
from jax.experimental import pallas as pl
from jax.experimental.pallas import tpu as pltpu
from jax.sharding import PartitionSpec as P

AXIS = "tensor"
HBM = pl.BlockSpec(memory_space=pl.ANY)
VMEM = pl.BlockSpec(memory_space=pltpu.VMEM)
SMEM = pl.BlockSpec(memory_space=pltpu.SMEM)
PARAMS = pltpu.CompilerParams(vmem_limit_bytes=32 * 1024 * 1024)


def largest_tile(extent, limit):
    tile = min(extent, limit)
    while extent % tile:
        tile //= 2
    return tile


def cost(flops, moved):
    return pl.CostEstimate(flops=flops, bytes_accessed=moved, transcendentals=0)


def team_of(n):
    return 2 if n % 2 == 0 else 1


def owner(me, slot, n):
    team = team_of(n)
    ahead = lax.rem(me + slot // team * team, n)
    if slot % team == 0:
        return ahead
    return ahead + 1 - 2 * lax.rem(ahead, 2)


def pre_block(ref, me, slot, n, rows):
    return ref[pl.ds(pl.multiple_of(owner(me, slot, n) * rows, rows), rows), :]


def stack(refs, starts, rows, columns=slice(None)):
    return jnp.concatenate([ref[s : s + rows, columns] for ref, s in zip(refs, starts)], axis=0)


def share(pre, grads, w_out_ref, w_in_ref, emit):
    back = jnp.dot(grads, w_out_ref[...], preferred_element_type=jnp.float32)
    hid = jnp.where(pre.astype(jnp.float32) > 0.0, back, 0.0).astype(jnp.bfloat16)
    width = w_in_ref.shape[0]
    tile = largest_tile(width, 512)
    for start in range(0, width, tile):
        columns = slice(start, start + tile)
        part = lax.dot_general(
            hid,
            w_in_ref[columns, :],
            (((1,), (1,)), ((), ())),
            preferred_element_type=jnp.float32,
        )
        emit(columns, part)
    return hid


def own_kernel(n, me_ref, pre_ref, w_out_ref, w_in_ref, grad_ref, inputs_ref, narrow_ref, hid_ref, part_ref):
    narrow_ref[...] = inputs_ref[...].astype(narrow_ref.dtype)

    def emit(columns, part):
        part_ref[:, columns] = part

    pre = pre_block(pre_ref, me_ref[0], 0, n, grad_ref.shape[0])
    hid_ref[...] = share(pre, grad_ref[...], w_out_ref, w_in_ref, emit)


def own_block(n, me, pre, w_out_t, w_in, grad, inputs):
    rows, width = grad.shape
    hidden = pre.shape[1]
    return pl.pallas_call(
        functools.partial(own_kernel, n),
        out_shape=[
            jax.ShapeDtypeStruct((rows, width), jnp.bfloat16),
            jax.ShapeDtypeStruct((rows, hidden), jnp.bfloat16),
            jax.ShapeDtypeStruct((rows, width), jnp.float32),
        ],
        in_specs=[SMEM] + [VMEM] * 5,
        out_specs=[VMEM] * 3,
        cost_estimate=cost(4 * rows * width * hidden, 4 * width * hidden + 12 * rows * width),
        compiler_params=PARAMS,
        name="own_block",
    )(me, pre, w_out_t, w_in, grad, inputs)


def partial_kernel(n, starts, me_ref, pre_ref, w_out_ref, w_in_ref, *refs):
    grad_refs, hid_ref, part_refs = refs[: n - 1], refs[n - 1], refs[n:]
    rows = part_refs[0].shape[0]
    me = me_ref[0]

    def emit(columns, part):
        part = part.astype(jnp.bfloat16)
        for k, ref in enumerate(part_refs):
            ref[:, columns] = part[k * rows : (k + 1) * rows]

    pre = jnp.concatenate([pre_block(pre_ref, me, k, n, rows) for k in range(1, n)], axis=0)
    hid_ref[...] = share(pre, stack(grad_refs, starts, rows), w_out_ref, w_in_ref, emit)


def partials(n, me, pre, w_out_t, w_in, pieces):
    hidden, width = pre.shape[1], w_in.shape[0]
    count = n - 1
    rows = pre.shape[0] // n
    grads, starts = zip(*pieces)
    return pl.pallas_call(
        functools.partial(partial_kernel, n, starts),
        out_shape=[jax.ShapeDtypeStruct((count * rows, hidden), jnp.bfloat16)]
        + [jax.ShapeDtypeStruct((rows, width), jnp.bfloat16)] * count,
        in_specs=[SMEM] + [VMEM] * (count + 3),
        out_specs=[VMEM] * (count + 1),
        cost_estimate=cost(
            4 * count * rows * width * hidden,
            4 * count * rows * (width + hidden) + 4 * width * hidden,
        ),
        compiler_params=PARAMS,
        name="partials",
    )(me, pre, w_out_t, w_in, *grads)


def weight_tiles(lefts, starts, right, out_hbm, buffer, sems):
    rows = right.shape[0] // len(lefts)
    moves = []
    for k in range(sems.shape[0]):
        tile = buffer.shape[0] // sems.shape[0]
        columns = slice(k * tile, (k + 1) * tile)
        buffer[columns, :] = lax.dot_general(
            stack(lefts, starts, rows, columns),
            right,
            (((0,), (0,)), ((), ())),
            preferred_element_type=jnp.float32,
        ).astype(buffer.dtype)
        moves.append(pltpu.make_async_copy(buffer.at[columns], out_hbm.at[columns], sems.at[k]))
        moves[k].start()
    return moves


def out_kernel(n, starts, me_ref, pre_ref, *refs):
    left_refs, (out_hbm, buffer, sems) = refs[:n], refs[n:]
    me, rows = me_ref[0], pre_ref.shape[0] // n
    pre = jnp.concatenate([pre_block(pre_ref, me, k, n, rows) for k in range(n)], axis=0)
    activ = jnp.maximum(pre, jnp.zeros_like(pre))
    for move in weight_tiles(left_refs, starts, activ, out_hbm, buffer, sems):
        move.wait()


def in_kernel(n, starts, hid_count, *refs):
    left_refs, hid_refs, (out_hbm, buffer, sems) = refs[:n], refs[n : n + hid_count], refs[n + hid_count :]
    hid = jnp.concatenate([ref[...] for ref in hid_refs], axis=0)
    for move in weight_tiles(left_refs, starts, hid, out_hbm, buffer, sems):
        move.wait()


def weight_scratch(width, hidden):
    return [
        pltpu.VMEM((width, hidden), jnp.bfloat16),
        pltpu.SemaphoreType.DMA((width // largest_tile(width, 256),)),
    ]


def weight_cost(total, width, hidden):
    return cost(2 * total * width * hidden, 2 * total * (width + hidden) + 2 * width * hidden)


def out_weight_grad(n, me, pieces, pre):
    lefts, starts = zip(*pieces)
    width, hidden = lefts[0].shape[1], pre.shape[1]
    return pl.pallas_call(
        functools.partial(out_kernel, n, starts),
        out_shape=jax.ShapeDtypeStruct((width, hidden), jnp.bfloat16),
        in_specs=[SMEM] + [VMEM] * (n + 1),
        out_specs=HBM,
        scratch_shapes=weight_scratch(width, hidden),
        cost_estimate=weight_cost(pre.shape[0], width, hidden),
        compiler_params=PARAMS,
        name="out_weight_grad",
    )(me, pre, *lefts)


def in_weight_grad(n, pieces, hids):
    lefts, starts = zip(*pieces)
    width, hidden = lefts[0].shape[1], hids[0].shape[1]
    return pl.pallas_call(
        functools.partial(in_kernel, n, starts, len(hids)),
        out_shape=jax.ShapeDtypeStruct((width, hidden), jnp.bfloat16),
        in_specs=[VMEM] * (n + len(hids)),
        out_specs=HBM,
        scratch_shapes=weight_scratch(width, hidden),
        cost_estimate=weight_cost(sum(hid.shape[0] for hid in hids), width, hidden),
        compiler_params=PARAMS,
        name="in_weight_grad",
    )(*lefts, *hids)


def owner_of(me, slot, n):
    ahead = (me + slot // team_of(n) * team_of(n)) % n
    return ahead ^ (slot % team_of(n))


def from_slot(n, block, slot):
    return lax.ppermute(block, AXIS, [(owner_of(i, slot, n), i) for i in range(n)])


def to_slot(n, block, slot):
    return lax.ppermute(block, AXIS, [(i, owner_of(i, slot, n)) for i in range(n)])


def later(values, *things):
    return lax.optimization_barrier((values, things))[0]


def on_device(inputs, out_grad, pre_saved, w_in, w_out_t, *, n):
    team = team_of(n)
    far = range(team, n, team)
    rows = inputs.shape[0]
    me = lax.axis_index(AXIS).astype(jnp.int32).reshape(1)
    grad_bf = out_grad.astype(jnp.bfloat16)
    grads, ins = {0: (grad_bf, 0)}, {}
    for k in reversed(range(1, n)):
        grads[k] = (from_slot(n, grad_bf, k), 0)
    inputs_bf, own_hid, input_grad = own_block(n, me, pre_saved, w_out_t, w_in, grad_bf, inputs)
    hids, ins[0] = [own_hid], (inputs_bf, 0)
    near = from_slot(n, inputs_bf, 1) if team == 2 else inputs_bf
    if team == 2:
        ins[1] = (near, 0)
    inputs_bf = later(inputs_bf, [grads[k][0] for k in range(1, n)])
    for k in far:
        got = from_slot(n, inputs_bf, k)
        ins[k] = (got, 0)
        if team == 2:
            ins[k + 1] = (from_slot(n, got, 1), 0)
    arrived = []
    if n > 1:
        hid, *parts = partials(n, me, pre_saved, w_out_t, w_in, [grads[k] for k in range(1, n)])
        parts, near = lax.optimization_barrier((parts, near))
        parts = [None] + parts
        hids.append(hid)
        if team == 2:
            ins[1] = (near, 0)
        sums = [parts[k] + from_slot(n, parts[k + 1], 1) if team == 2 else parts[k] for k in far]
        sums, parts = lax.optimization_barrier((sums, parts))
        arrived = [to_slot(n, block, k) for k, block in zip(far, sums)]
        if team == 2:
            arrived.append(from_slot(n, parts[1], 1))
    grad_w_out_t = out_weight_grad(n, me, [grads[k] for k in range(n)], pre_saved)
    grad_w_in = in_weight_grad(n, [ins[k] for k in range(n)], hids)
    for block in later(arrived, grad_w_in):
        input_grad = input_grad + block.astype(jnp.float32)
    return (input_grad, grad_w_in, grad_w_out_t)


def solution(mesh):
    in_specs = (
        P(("dp", AXIS), None),
        P(("dp", AXIS), None),
        P("dp", AXIS),
        P(None, AXIS),
        P(None, AXIS),
    )
    out_specs = (P(("dp", AXIS), None), P("dp", AXIS), P("dp", AXIS))
    return jax.shard_map(
        functools.partial(on_device, n=mesh.shape[AXIS]),
        mesh=mesh,
        in_specs=in_specs,
        out_specs=out_specs,
        check_vma=False,
    )
```

```python
import functools

import jax
import jax.numpy as jnp
from jax import lax
from jax.experimental import pallas as pl
from jax.experimental.pallas import tpu as pltpu
from jax.sharding import PartitionSpec as P

AXIS = "tensor"
HBM = pl.BlockSpec(memory_space=pl.ANY)
VMEM = pl.BlockSpec(memory_space=pltpu.VMEM)
SMEM = pl.BlockSpec(memory_space=pltpu.SMEM)
PARAMS = pltpu.CompilerParams(vmem_limit_bytes=32 * 1024 * 1024)


def largest_tile(extent, limit):
    tile = min(extent, limit)
    while extent % tile:
        tile //= 2
    return tile


def cost(flops, moved):
    return pl.CostEstimate(flops=flops, bytes_accessed=moved, transcendentals=0)


def team_of(n):
    return 2 if n % 2 == 0 else 1


def owner(me, slot, n):
    team = team_of(n)
    ahead = lax.rem(me + slot // team * team, n)
    if slot % team == 0:
        return ahead
    return ahead + 1 - 2 * lax.rem(ahead, 2)


def pre_block(ref, me, slot, n, rows):
    return ref[pl.ds(pl.multiple_of(owner(me, slot, n) * rows, rows), rows), :]


def stack(refs, starts, rows, columns=slice(None)):
    return jnp.concatenate([ref[s : s + rows, columns] for ref, s in zip(refs, starts)], axis=0)


def pair_kernel(upper_ref, lower_ref, both_ref):
    rows = upper_ref.shape[0]
    both_ref[:rows, :] = upper_ref[...]
    both_ref[rows:, :] = lower_ref[...].astype(both_ref.dtype)


def pair(upper, lower):
    rows, width = upper.shape
    return pl.pallas_call(
        pair_kernel,
        out_shape=jax.ShapeDtypeStruct((2 * rows, width), upper.dtype),
        in_specs=[VMEM] * 2,
        out_specs=VMEM,
        cost_estimate=cost(0, 10 * rows * width),
        compiler_params=PARAMS,
        name="pair",
    )(upper, lower)


def share(pre, grads, w_out_ref, w_in_ref, emit):
    back = jnp.dot(grads, w_out_ref[...], preferred_element_type=jnp.float32)
    hid = jnp.where(pre.astype(jnp.float32) > 0.0, back, 0.0).astype(jnp.bfloat16)
    width = w_in_ref.shape[0]
    tile = largest_tile(width, 512)
    for start in range(0, width, tile):
        columns = slice(start, start + tile)
        part = lax.dot_general(
            hid,
            w_in_ref[columns, :],
            (((1,), (1,)), ((), ())),
            preferred_element_type=jnp.float32,
        )
        emit(columns, part)
    return hid


def own_kernel(n, me_ref, pre_ref, w_out_ref, w_in_ref, grad_ref, hid_ref, part_ref):
    rows = part_ref.shape[0]

    def emit(columns, part):
        part_ref[:, columns] = part

    pre = pre_block(pre_ref, me_ref[0], 0, n, rows)
    hid_ref[...] = share(pre, grad_ref[...], w_out_ref, w_in_ref, emit)


def own_block(n, me, pre, w_out_t, w_in, grad):
    hidden, width = pre.shape[1], w_in.shape[0]
    rows = pre.shape[0] // n
    return pl.pallas_call(
        functools.partial(own_kernel, n),
        out_shape=[
            jax.ShapeDtypeStruct((rows, hidden), jnp.bfloat16),
            jax.ShapeDtypeStruct((rows, width), jnp.float32),
        ],
        in_specs=[SMEM] + [VMEM] * 4,
        out_specs=[VMEM] * 2,
        cost_estimate=cost(4 * rows * width * hidden, 4 * width * hidden + 6 * rows * width),
        compiler_params=PARAMS,
        name="own_block",
    )(me, pre, w_out_t, w_in, grad)


def partial_kernel(n, starts, me_ref, pre_ref, w_out_ref, w_in_ref, *refs):
    grad_refs, hid_ref, part_refs = refs[: n - 1], refs[n - 1], refs[n:]
    rows = part_refs[0].shape[0]
    me = me_ref[0]

    def emit(columns, part):
        part = part.astype(jnp.bfloat16)
        for k, ref in enumerate(part_refs):
            ref[:, columns] = part[k * rows : (k + 1) * rows]

    pre = jnp.concatenate([pre_block(pre_ref, me, k, n, rows) for k in range(1, n)], axis=0)
    hid_ref[...] = share(pre, stack(grad_refs, starts, rows), w_out_ref, w_in_ref, emit)


def partials(n, me, pre, w_out_t, w_in, pieces):
    hidden, width = pre.shape[1], w_in.shape[0]
    count = n - 1
    rows = pre.shape[0] // n
    grads, starts = zip(*pieces)
    return pl.pallas_call(
        functools.partial(partial_kernel, n, starts),
        out_shape=[jax.ShapeDtypeStruct((count * rows, hidden), jnp.bfloat16)]
        + [jax.ShapeDtypeStruct((rows, width), jnp.bfloat16)] * count,
        in_specs=[SMEM] + [VMEM] * (count + 3),
        out_specs=[VMEM] * (count + 1),
        cost_estimate=cost(
            4 * count * rows * width * hidden,
            4 * count * rows * (width + hidden) + 4 * width * hidden,
        ),
        compiler_params=PARAMS,
        name="partials",
    )(me, pre, w_out_t, w_in, *grads)


def weight_tiles(lefts, starts, right, out_hbm, buffer, sems):
    rows = right.shape[0] // len(lefts)
    moves = []
    for k in range(sems.shape[0]):
        tile = buffer.shape[0] // sems.shape[0]
        columns = slice(k * tile, (k + 1) * tile)
        buffer[columns, :] = lax.dot_general(
            stack(lefts, starts, rows, columns),
            right,
            (((0,), (0,)), ((), ())),
            preferred_element_type=jnp.float32,
        ).astype(buffer.dtype)
        moves.append(pltpu.make_async_copy(buffer.at[columns], out_hbm.at[columns], sems.at[k]))
        moves[k].start()
    return moves


def out_kernel(n, starts, me_ref, pre_ref, *refs):
    left_refs, (out_hbm, buffer, sems) = refs[:n], refs[n:]
    me, rows = me_ref[0], pre_ref.shape[0] // n
    pre = jnp.concatenate([pre_block(pre_ref, me, k, n, rows) for k in range(n)], axis=0)
    activ = jnp.maximum(pre, jnp.zeros_like(pre))
    for move in weight_tiles(left_refs, starts, activ, out_hbm, buffer, sems):
        move.wait()


def in_kernel(n, starts, hid_count, *refs):
    left_refs, hid_refs, (out_hbm, buffer, sems) = refs[:n], refs[n : n + hid_count], refs[n + hid_count :]
    hid = jnp.concatenate([ref[...] for ref in hid_refs], axis=0)
    for move in weight_tiles(left_refs, starts, hid, out_hbm, buffer, sems):
        move.wait()


def weight_scratch(width, hidden):
    return [
        pltpu.VMEM((width, hidden), jnp.bfloat16),
        pltpu.SemaphoreType.DMA((width // largest_tile(width, 256),)),
    ]


def weight_cost(total, width, hidden):
    return cost(2 * total * width * hidden, 2 * total * (width + hidden) + 2 * width * hidden)


def out_weight_grad(n, me, pieces, pre):
    lefts, starts = zip(*pieces)
    width, hidden = lefts[0].shape[1], pre.shape[1]
    return pl.pallas_call(
        functools.partial(out_kernel, n, starts),
        out_shape=jax.ShapeDtypeStruct((width, hidden), jnp.bfloat16),
        in_specs=[SMEM] + [VMEM] * (n + 1),
        out_specs=HBM,
        scratch_shapes=weight_scratch(width, hidden),
        cost_estimate=weight_cost(pre.shape[0], width, hidden),
        compiler_params=PARAMS,
        name="out_weight_grad",
    )(me, pre, *lefts)


def in_weight_grad(n, pieces, hids):
    lefts, starts = zip(*pieces)
    width, hidden = lefts[0].shape[1], hids[0].shape[1]
    return pl.pallas_call(
        functools.partial(in_kernel, n, starts, len(hids)),
        out_shape=jax.ShapeDtypeStruct((width, hidden), jnp.bfloat16),
        in_specs=[VMEM] * (n + len(hids)),
        out_specs=HBM,
        scratch_shapes=weight_scratch(width, hidden),
        cost_estimate=weight_cost(sum(hid.shape[0] for hid in hids), width, hidden),
        compiler_params=PARAMS,
        name="in_weight_grad",
    )(*lefts, *hids)


def sum_kernel(part_ref, *refs):
    arrived_refs, (sum_hbm, buffer, sems) = refs[:-3], refs[-3:]
    tile = buffer.shape[1] // sems.shape[0]
    moves = []
    for k in range(sems.shape[0]):
        columns = slice(k * tile, (k + 1) * tile)
        total = part_ref[:, columns]
        for ref in arrived_refs:
            total = total + ref[:, columns].astype(jnp.float32)
        buffer[:, columns] = total
        moves.append(pltpu.make_async_copy(buffer.at[:, columns], sum_hbm.at[:, columns], sems.at[k]))
        moves[k].start()
    for move in moves:
        move.wait()


def summed(part, arrived):
    rows, width = part.shape
    return pl.pallas_call(
        sum_kernel,
        out_shape=jax.ShapeDtypeStruct(part.shape, jnp.float32),
        in_specs=[VMEM] * (1 + len(arrived)),
        out_specs=HBM,
        scratch_shapes=[
            pltpu.VMEM(part.shape, jnp.float32),
            pltpu.SemaphoreType.DMA((width // largest_tile(width, 512),)),
        ],
        cost_estimate=cost(len(arrived) * rows * width, (8 + 2 * len(arrived)) * rows * width),
        compiler_params=PARAMS,
        name="sum",
    )(part, *arrived)


def owner_of(me, slot, n):
    ahead = (me + slot // team_of(n) * team_of(n)) % n
    return ahead ^ (slot % team_of(n))


def from_slot(n, block, slot):
    return lax.ppermute(block, AXIS, [(owner_of(i, slot, n), i) for i in range(n)])


def to_slot(n, block, slot):
    return lax.ppermute(block, AXIS, [(i, owner_of(i, slot, n)) for i in range(n)])


def later(values, *things):
    return lax.optimization_barrier((values, things))[0]


def on_device(inputs, out_grad, pre_saved, w_in, w_out_t, *, n):
    team = team_of(n)
    far = range(team, n, team)
    rows = inputs.shape[0]
    me = lax.axis_index(AXIS).astype(jnp.int32).reshape(1)
    grad_bf = out_grad.astype(jnp.bfloat16)
    far_grads = [from_slot(n, grad_bf, k) for k in far]
    both = pair(grad_bf, inputs)
    grads, ins = {0: (grad_bf, 0)}, {}
    if team == 2:
        near = from_slot(n, both, 1)
        grads[1], ins[1] = (near, 0), (near, rows)
    own_hid, input_grad = own_block(n, me, pre_saved, w_out_t, w_in, grad_bf)
    hids = [own_hid]
    far_grads = later(far_grads, own_hid)
    for k, got in zip(far, far_grads):
        grads[k] = (got, 0)
        if team == 2:
            grads[k + 1] = (from_slot(n, got, 1), 0)
    inputs_bf = later(inputs, far_grads).astype(jnp.bfloat16)
    ins[0] = (inputs_bf, 0)
    far_ins = [from_slot(n, inputs_bf, k) for k in far]
    arrived, pre = [], pre_saved
    if n > 1:
        hid, *parts = partials(n, me, pre_saved, w_out_t, w_in, [grads[k] for k in range(1, n)])
        pre = later(pre, parts)
        parts = [None] + parts
        hids.append(hid)
        sums = [parts[k] + from_slot(n, parts[k + 1], 1) if team == 2 else parts[k] for k in far]
        sums, parts = lax.optimization_barrier((sums, parts))
        arrived = [to_slot(n, block, k) for k, block in zip(far, sums)]
        if team == 2:
            arrived.append(from_slot(n, parts[1], 1))
    grad_w_out_t = out_weight_grad(n, me, [grads[k] for k in range(n)], pre)
    far_ins = later(far_ins, grad_w_out_t)
    for k, got in zip(far, far_ins):
        ins[k] = (got, 0)
        if team == 2:
            ins[k + 1] = (from_slot(n, got, 1), 0)
    grad_w_in = in_weight_grad(n, [ins[k] for k in range(n)], hids)
    return (summed(input_grad, arrived), grad_w_in, grad_w_out_t)


def solution(mesh):
    in_specs = (
        P(("dp", AXIS), None),
        P(("dp", AXIS), None),
        P("dp", AXIS),
        P(None, AXIS),
        P(None, AXIS),
    )
    out_specs = (P(("dp", AXIS), None), P("dp", AXIS), P("dp", AXIS))
    return jax.shard_map(
        functools.partial(on_device, n=mesh.shape[AXIS]),
        mesh=mesh,
        in_specs=in_specs,
        out_specs=out_specs,
        check_vma=False,
    )
```

```python
import functools

import jax
import jax.numpy as jnp
from jax import lax
from jax.experimental import pallas as pl
from jax.experimental.pallas import tpu as pltpu
from jax.sharding import PartitionSpec as P

AXIS = "tensor"
HBM = pl.BlockSpec(memory_space=pl.ANY)
VMEM = pl.BlockSpec(memory_space=pltpu.VMEM)
SMEM = pl.BlockSpec(memory_space=pltpu.SMEM)
PARAMS = pltpu.CompilerParams(vmem_limit_bytes=32 * 1024 * 1024)


def largest_tile(extent, limit):
    tile = min(extent, limit)
    while extent % tile:
        tile //= 2
    return tile


def cost(flops, moved):
    return pl.CostEstimate(flops=flops, bytes_accessed=moved, transcendentals=0)


def team_of(n):
    return 2 if n % 2 == 0 else 1


def crosses(slot, n):
    return team_of(n) == 2 and (slot % 2 == 1) == (slot < 2)


def owner(me, slot, n):
    team = team_of(n)
    ahead = lax.rem(me + slot // team * team, n)
    return ahead + 1 - 2 * lax.rem(ahead, 2) if crosses(slot, n) else ahead


def pre_block(ref, me, slot, n, rows):
    return ref[pl.ds(pl.multiple_of(owner(me, slot, n) * rows, rows), rows), :]


def stack(refs, starts, rows, columns=slice(None)):
    return jnp.concatenate([ref[s : s + rows, columns] for ref, s in zip(refs, starts)], axis=0)


def pair_kernel(upper_ref, lower_ref, both_ref):
    rows = upper_ref.shape[0]
    both_ref[:rows, :] = upper_ref[...]
    both_ref[rows:, :] = lower_ref[...].astype(both_ref.dtype)


def pair(upper, lower):
    rows, width = upper.shape
    return pl.pallas_call(
        pair_kernel,
        out_shape=jax.ShapeDtypeStruct((2 * rows, width), upper.dtype),
        in_specs=[VMEM] * 2,
        out_specs=VMEM,
        cost_estimate=cost(0, 10 * rows * width),
        compiler_params=PARAMS,
        name="pair",
    )(upper, lower)


def share(pre, grads, w_out_ref, w_in_ref, emit):
    back = jnp.dot(grads, w_out_ref[...], preferred_element_type=jnp.float32)
    hid = jnp.where(pre.astype(jnp.float32) > 0.0, back, 0.0).astype(jnp.bfloat16)
    width = w_in_ref.shape[0]
    tile = largest_tile(width, 512)
    for start in range(0, width, tile):
        columns = slice(start, start + tile)
        part = lax.dot_general(
            hid,
            w_in_ref[columns, :],
            (((1,), (1,)), ((), ())),
            preferred_element_type=jnp.float32,
        )
        emit(columns, part)
    return hid


def own_kernel(n, me_ref, pre_ref, w_out_ref, w_in_ref, grad_ref, hid_ref, part_ref):
    rows = part_ref.shape[0]

    def emit(columns, part):
        part_ref[:, columns] = part

    pre = pre_block(pre_ref, me_ref[0], 0, n, rows)
    hid_ref[...] = share(pre, grad_ref[...], w_out_ref, w_in_ref, emit)


def own_block(n, me, pre, w_out_t, w_in, grad):
    hidden, width = pre.shape[1], w_in.shape[0]
    rows = pre.shape[0] // n
    return pl.pallas_call(
        functools.partial(own_kernel, n),
        out_shape=[
            jax.ShapeDtypeStruct((rows, hidden), jnp.bfloat16),
            jax.ShapeDtypeStruct((rows, width), jnp.float32),
        ],
        in_specs=[SMEM] + [VMEM] * 4,
        out_specs=[VMEM] * 2,
        cost_estimate=cost(4 * rows * width * hidden, 4 * width * hidden + 6 * rows * width),
        compiler_params=PARAMS,
        name="own_block",
    )(me, pre, w_out_t, w_in, grad)


def partial_kernel(n, starts, me_ref, pre_ref, w_out_ref, w_in_ref, *refs):
    grad_refs, hid_ref, part_refs = refs[: n - 1], refs[n - 1], refs[n:]
    rows = part_refs[0].shape[0]
    me = me_ref[0]

    def emit(columns, part):
        part = part.astype(jnp.bfloat16)
        for k, ref in enumerate(part_refs):
            ref[:, columns] = part[k * rows : (k + 1) * rows]

    pre = jnp.concatenate([pre_block(pre_ref, me, k, n, rows) for k in range(1, n)], axis=0)
    hid_ref[...] = share(pre, stack(grad_refs, starts, rows), w_out_ref, w_in_ref, emit)


def partials(n, me, pre, w_out_t, w_in, pieces):
    hidden, width = pre.shape[1], w_in.shape[0]
    count = n - 1
    rows = pre.shape[0] // n
    grads, starts = zip(*pieces)
    return pl.pallas_call(
        functools.partial(partial_kernel, n, starts),
        out_shape=[jax.ShapeDtypeStruct((count * rows, hidden), jnp.bfloat16)]
        + [jax.ShapeDtypeStruct((rows, width), jnp.bfloat16)] * count,
        in_specs=[SMEM] + [VMEM] * (count + 3),
        out_specs=[VMEM] * (count + 1),
        cost_estimate=cost(
            4 * count * rows * width * hidden,
            4 * count * rows * (width + hidden) + 4 * width * hidden,
        ),
        compiler_params=PARAMS,
        name="partials",
    )(me, pre, w_out_t, w_in, *grads)


def weight_tiles(lefts, starts, right, out_hbm, buffer, sems):
    rows = right.shape[0] // len(lefts)
    moves = []
    for k in range(sems.shape[0]):
        tile = buffer.shape[0] // sems.shape[0]
        columns = slice(k * tile, (k + 1) * tile)
        buffer[columns, :] = lax.dot_general(
            stack(lefts, starts, rows, columns),
            right,
            (((0,), (0,)), ((), ())),
            preferred_element_type=jnp.float32,
        ).astype(buffer.dtype)
        moves.append(pltpu.make_async_copy(buffer.at[columns], out_hbm.at[columns], sems.at[k]))
        moves[k].start()
    return moves


def out_kernel(n, starts, me_ref, pre_ref, *refs):
    left_refs, (out_hbm, buffer, sems) = refs[:n], refs[n:]
    me, rows = me_ref[0], pre_ref.shape[0] // n
    pre = jnp.concatenate([pre_block(pre_ref, me, k, n, rows) for k in range(n)], axis=0)
    activ = jnp.maximum(pre, jnp.zeros_like(pre))
    for move in weight_tiles(left_refs, starts, activ, out_hbm, buffer, sems):
        move.wait()


def in_kernel(n, starts, hid_count, *refs):
    left_refs, hid_refs, (out_hbm, buffer, sems) = refs[:n], refs[n : n + hid_count], refs[n + hid_count :]
    hid = jnp.concatenate([ref[...] for ref in hid_refs], axis=0)
    for move in weight_tiles(left_refs, starts, hid, out_hbm, buffer, sems):
        move.wait()


def weight_scratch(width, hidden):
    return [
        pltpu.VMEM((width, hidden), jnp.bfloat16),
        pltpu.SemaphoreType.DMA((width // largest_tile(width, 256),)),
    ]


def weight_cost(total, width, hidden):
    return cost(2 * total * width * hidden, 2 * total * (width + hidden) + 2 * width * hidden)


def out_weight_grad(n, me, pieces, pre):
    lefts, starts = zip(*pieces)
    width, hidden = lefts[0].shape[1], pre.shape[1]
    return pl.pallas_call(
        functools.partial(out_kernel, n, starts),
        out_shape=jax.ShapeDtypeStruct((width, hidden), jnp.bfloat16),
        in_specs=[SMEM] + [VMEM] * (n + 1),
        out_specs=HBM,
        scratch_shapes=weight_scratch(width, hidden),
        cost_estimate=weight_cost(pre.shape[0], width, hidden),
        compiler_params=PARAMS,
        name="out_weight_grad",
    )(me, pre, *lefts)


def in_weight_grad(n, pieces, hids):
    lefts, starts = zip(*pieces)
    width, hidden = lefts[0].shape[1], hids[0].shape[1]
    return pl.pallas_call(
        functools.partial(in_kernel, n, starts, len(hids)),
        out_shape=jax.ShapeDtypeStruct((width, hidden), jnp.bfloat16),
        in_specs=[VMEM] * (n + len(hids)),
        out_specs=HBM,
        scratch_shapes=weight_scratch(width, hidden),
        cost_estimate=weight_cost(sum(hid.shape[0] for hid in hids), width, hidden),
        compiler_params=PARAMS,
        name="in_weight_grad",
    )(*lefts, *hids)


def owner_of(me, slot, n):
    ahead = (me + slot // team_of(n) * team_of(n)) % n
    return ahead ^ int(crosses(slot, n))


def from_slot(n, block, slot):
    return lax.ppermute(block, AXIS, [(owner_of(i, slot, n), i) for i in range(n)])


def to_slot(n, block, slot):
    return lax.ppermute(block, AXIS, [(i, owner_of(i, slot, n)) for i in range(n)])


def later(values, *things):
    return lax.optimization_barrier((values, things))[0]


def on_device(inputs, out_grad, pre_saved, w_in, w_out_t, *, n):
    team = team_of(n)
    far = range(team, n, team)
    rows = inputs.shape[0]
    me = lax.axis_index(AXIS).astype(jnp.int32).reshape(1)
    grad_bf = out_grad.astype(jnp.bfloat16)
    far_grads = [from_slot(n, grad_bf, k) for k in far]
    both = pair(grad_bf, inputs)
    grads, ins = {0: (grad_bf, 0)}, {}
    if team == 2:
        near = from_slot(n, both, 1)
        grads[1], ins[1] = (near, 0), (near, rows)
    own_hid, input_grad = own_block(n, me, pre_saved, w_out_t, w_in, grad_bf)
    hids = [own_hid]
    far_grads = later(far_grads, own_hid)
    for k, got in zip(far, far_grads):
        grads[k] = (got, 0)
        if team == 2:
            grads[k + 1] = (from_slot(n, got, 1), 0)
    inputs_bf = later(inputs, far_grads).astype(jnp.bfloat16)
    ins[0] = (inputs_bf, 0)
    far_ins = [from_slot(n, inputs_bf, k) for k in far]
    arrived, pre = [], pre_saved
    if n > 1:
        hid, *parts = partials(n, me, pre_saved, w_out_t, w_in, [grads[k] for k in range(1, n)])
        pre = later(pre, parts)
        parts = [None] + parts
        hids.append(hid)
        sums = [parts[k] + from_slot(n, parts[k + 1], 1) if team == 2 else parts[k] for k in far]
        sums, parts = lax.optimization_barrier((sums, parts))
        arrived = [to_slot(n, block, k) for k, block in zip(far, sums)]
        if team == 2:
            arrived.append(from_slot(n, parts[1], 1))
    grad_w_out_t = out_weight_grad(n, me, [grads[k] for k in range(n)], pre)
    far_ins = later(far_ins, grad_w_out_t)
    for k, got in zip(far, far_ins):
        ins[k] = (got, 0)
        if team == 2:
            ins[k + 1] = (from_slot(n, got, 1), 0)
    grad_w_in = in_weight_grad(n, [ins[k] for k in range(n)], hids)
    for block in arrived:
        input_grad = input_grad + block.astype(jnp.float32)
    return (input_grad, grad_w_in, grad_w_out_t)


def solution(mesh):
    in_specs = (
        P(("dp", AXIS), None),
        P(("dp", AXIS), None),
        P("dp", AXIS),
        P(None, AXIS),
        P(None, AXIS),
    )
    out_specs = (P(("dp", AXIS), None), P("dp", AXIS), P("dp", AXIS))
    return jax.shard_map(
        functools.partial(on_device, n=mesh.shape[AXIS]),
        mesh=mesh,
        in_specs=in_specs,
        out_specs=out_specs,
        check_vma=False,
    )
```

```python
import functools

import jax
import jax.numpy as jnp
from jax import lax
from jax.experimental import pallas as pl
from jax.experimental.pallas import tpu as pltpu
from jax.sharding import PartitionSpec as P

AXIS = "tensor"
HBM = pl.BlockSpec(memory_space=pl.ANY)
VMEM = pl.BlockSpec(memory_space=pltpu.VMEM)
SMEM = pl.BlockSpec(memory_space=pltpu.SMEM)
PARAMS = pltpu.CompilerParams(vmem_limit_bytes=32 * 1024 * 1024)


def largest_tile(extent, limit):
    tile = min(extent, limit)
    while extent % tile:
        tile //= 2
    return tile


def cost(flops, moved):
    return pl.CostEstimate(flops=flops, bytes_accessed=moved, transcendentals=0)


def team_of(n):
    return 2 if n % 2 == 0 else 1


def crosses(slot, n):
    return team_of(n) == 2 and (slot % 2 == 1) == (slot < 2)


def owner(me, slot, n):
    team = team_of(n)
    ahead = lax.rem(me + slot // team * team, n)
    return ahead + 1 - 2 * lax.rem(ahead, 2) if crosses(slot, n) else ahead


def pre_block(ref, me, slot, n, rows):
    return ref[pl.ds(pl.multiple_of(owner(me, slot, n) * rows, rows), rows), :]


def stack(refs, starts, rows, columns=slice(None)):
    return jnp.concatenate([ref[s : s + rows, columns] for ref, s in zip(refs, starts)], axis=0)


def share(pre, grads, w_out_ref, w_in_ref, emit):
    back = jnp.dot(grads, w_out_ref[...], preferred_element_type=jnp.float32)
    hid = jnp.where(pre.astype(jnp.float32) > 0.0, back, 0.0).astype(jnp.bfloat16)
    width = w_in_ref.shape[0]
    tile = largest_tile(width, 512)
    for start in range(0, width, tile):
        columns = slice(start, start + tile)
        part = lax.dot_general(
            hid,
            w_in_ref[columns, :],
            (((1,), (1,)), ((), ())),
            preferred_element_type=jnp.float32,
        )
        emit(columns, part)
    return hid


def own_kernel(n, me_ref, pre_ref, w_out_ref, w_in_ref, grad_ref, hid_ref, part_ref):
    rows = part_ref.shape[0]

    def emit(columns, part):
        part_ref[:, columns] = part

    pre = pre_block(pre_ref, me_ref[0], 0, n, rows)
    hid_ref[...] = share(pre, grad_ref[...], w_out_ref, w_in_ref, emit)


def own_block(n, me, pre, w_out_t, w_in, grad):
    hidden, width = pre.shape[1], w_in.shape[0]
    rows = pre.shape[0] // n
    return pl.pallas_call(
        functools.partial(own_kernel, n),
        out_shape=[
            jax.ShapeDtypeStruct((rows, hidden), jnp.bfloat16),
            jax.ShapeDtypeStruct((rows, width), jnp.float32),
        ],
        in_specs=[SMEM] + [VMEM] * 4,
        out_specs=[VMEM] * 2,
        cost_estimate=cost(4 * rows * width * hidden, 4 * width * hidden + 6 * rows * width),
        compiler_params=PARAMS,
        name="own_block",
    )(me, pre, w_out_t, w_in, grad)


def partial_kernel(n, starts, me_ref, pre_ref, w_out_ref, w_in_ref, *refs):
    grad_refs, hid_ref, part_refs = refs[: n - 1], refs[n - 1], refs[n:]
    rows = part_refs[0].shape[0]
    me = me_ref[0]

    def emit(columns, part):
        part = part.astype(jnp.bfloat16)
        for k, ref in enumerate(part_refs):
            ref[:, columns] = part[k * rows : (k + 1) * rows]

    pre = jnp.concatenate([pre_block(pre_ref, me, k, n, rows) for k in range(1, n)], axis=0)
    hid_ref[...] = share(pre, stack(grad_refs, starts, rows), w_out_ref, w_in_ref, emit)


def partials(n, me, pre, w_out_t, w_in, pieces):
    hidden, width = pre.shape[1], w_in.shape[0]
    count = n - 1
    rows = pre.shape[0] // n
    grads, starts = zip(*pieces)
    return pl.pallas_call(
        functools.partial(partial_kernel, n, starts),
        out_shape=[jax.ShapeDtypeStruct((count * rows, hidden), jnp.bfloat16)]
        + [jax.ShapeDtypeStruct((rows, width), jnp.bfloat16)] * count,
        in_specs=[SMEM] + [VMEM] * (count + 3),
        out_specs=[VMEM] * (count + 1),
        cost_estimate=cost(
            4 * count * rows * width * hidden,
            4 * count * rows * (width + hidden) + 4 * width * hidden,
        ),
        compiler_params=PARAMS,
        name="partials",
    )(me, pre, w_out_t, w_in, *grads)


def weight_tiles(lefts, starts, right, out_hbm, buffer, sems):
    rows = right.shape[0] // len(lefts)
    moves = []
    for k in range(sems.shape[0]):
        tile = buffer.shape[0] // sems.shape[0]
        columns = slice(k * tile, (k + 1) * tile)
        buffer[columns, :] = lax.dot_general(
            stack(lefts, starts, rows, columns),
            right,
            (((0,), (0,)), ((), ())),
            preferred_element_type=jnp.float32,
        ).astype(buffer.dtype)
        moves.append(pltpu.make_async_copy(buffer.at[columns], out_hbm.at[columns], sems.at[k]))
        moves[k].start()
    return moves


def out_kernel(n, starts, me_ref, pre_ref, *refs):
    left_refs, (out_hbm, buffer, sems) = refs[:n], refs[n:]
    me, rows = me_ref[0], pre_ref.shape[0] // n
    pre = jnp.concatenate([pre_block(pre_ref, me, k, n, rows) for k in range(n)], axis=0)
    activ = jnp.maximum(pre, jnp.zeros_like(pre))
    for move in weight_tiles(left_refs, starts, activ, out_hbm, buffer, sems):
        move.wait()


def in_kernel(n, starts, hid_count, *refs):
    left_refs, hid_refs, (out_hbm, buffer, sems) = refs[:n], refs[n : n + hid_count], refs[n + hid_count :]
    hid = jnp.concatenate([ref[...] for ref in hid_refs], axis=0)
    for move in weight_tiles(left_refs, starts, hid, out_hbm, buffer, sems):
        move.wait()


def weight_scratch(width, hidden):
    return [
        pltpu.VMEM((width, hidden), jnp.bfloat16),
        pltpu.SemaphoreType.DMA((width // largest_tile(width, 256),)),
    ]


def weight_cost(total, width, hidden):
    return cost(2 * total * width * hidden, 2 * total * (width + hidden) + 2 * width * hidden)


def out_weight_grad(n, me, pieces, pre):
    lefts, starts = zip(*pieces)
    width, hidden = lefts[0].shape[1], pre.shape[1]
    return pl.pallas_call(
        functools.partial(out_kernel, n, starts),
        out_shape=jax.ShapeDtypeStruct((width, hidden), jnp.bfloat16),
        in_specs=[SMEM] + [VMEM] * (n + 1),
        out_specs=HBM,
        scratch_shapes=weight_scratch(width, hidden),
        cost_estimate=weight_cost(pre.shape[0], width, hidden),
        compiler_params=PARAMS,
        name="out_weight_grad",
    )(me, pre, *lefts)


def in_weight_grad(n, pieces, hids):
    lefts, starts = zip(*pieces)
    width, hidden = lefts[0].shape[1], hids[0].shape[1]
    return pl.pallas_call(
        functools.partial(in_kernel, n, starts, len(hids)),
        out_shape=jax.ShapeDtypeStruct((width, hidden), jnp.bfloat16),
        in_specs=[VMEM] * (n + len(hids)),
        out_specs=HBM,
        scratch_shapes=weight_scratch(width, hidden),
        cost_estimate=weight_cost(sum(hid.shape[0] for hid in hids), width, hidden),
        compiler_params=PARAMS,
        name="in_weight_grad",
    )(*lefts, *hids)


def owner_of(me, slot, n):
    ahead = (me + slot // team_of(n) * team_of(n)) % n
    return ahead ^ int(crosses(slot, n))


def from_slot(n, block, slot):
    return lax.ppermute(block, AXIS, [(owner_of(i, slot, n), i) for i in range(n)])


def to_slot(n, block, slot):
    return lax.ppermute(block, AXIS, [(i, owner_of(i, slot, n)) for i in range(n)])


def later(values, *things):
    return lax.optimization_barrier((values, things))[0]


def on_device(inputs, out_grad, pre_saved, w_in, w_out_t, *, n):
    team = team_of(n)
    far = range(team, n, team)
    me = lax.axis_index(AXIS).astype(jnp.int32).reshape(1)
    grad_bf = out_grad.astype(jnp.bfloat16)
    far_grads = [from_slot(n, grad_bf, k) for k in far]
    grads, ins = {0: (grad_bf, 0)}, {}
    if team == 2:
        grads[1] = (from_slot(n, grad_bf, 1), 0)
    own_hid, input_grad = own_block(n, me, pre_saved, w_out_t, w_in, grad_bf)
    hids = [own_hid]
    far_grads = later(far_grads, own_hid)
    for k, got in zip(far, far_grads):
        grads[k] = (got, 0)
        if team == 2:
            grads[k + 1] = (from_slot(n, got, 1), 0)
    inputs_bf = later(inputs, far_grads).astype(jnp.bfloat16)
    ins[0] = (inputs_bf, 0)
    far_ins = [from_slot(n, inputs_bf, k) for k in far]
    near = from_slot(n, inputs_bf, 1) if team == 2 else inputs_bf
    arrived, pre = [], pre_saved
    if n > 1:
        hid, *parts = partials(n, me, pre_saved, w_out_t, w_in, [grads[k] for k in range(1, n)])
        near, pre = lax.optimization_barrier((near, later(pre, parts, far_ins)))
        if team == 2:
            ins[1] = (near, 0)
        parts = [None] + parts
        hids.append(hid)
        grad_w_out_t = out_weight_grad(n, me, [grads[k] for k in range(n)], pre)
        sums = [parts[k] + from_slot(n, parts[k + 1], 1) if team == 2 else parts[k] for k in far]
        sums, parts, far_ins, grad_w_out_t = lax.optimization_barrier(
            (sums, parts, far_ins, grad_w_out_t)
        )
        arrived = [to_slot(n, block, k) for k, block in zip(far, sums)]
        if team == 2:
            arrived.append(from_slot(n, parts[1], 1))
    else:
        grad_w_out_t = out_weight_grad(n, me, [grads[0]], pre)
    for k, got in zip(far, far_ins):
        ins[k] = (got, 0)
        if team == 2:
            ins[k + 1] = (from_slot(n, got, 1), 0)
    grad_w_in = in_weight_grad(n, [ins[k] for k in range(n)], hids)
    for block in later(arrived, grad_w_in):
        input_grad = input_grad + block.astype(jnp.float32)
    return (input_grad, grad_w_in, grad_w_out_t)


def solution(mesh):
    in_specs = (
        P(("dp", AXIS), None),
        P(("dp", AXIS), None),
        P("dp", AXIS),
        P(None, AXIS),
        P(None, AXIS),
    )
    out_specs = (P(("dp", AXIS), None), P("dp", AXIS), P("dp", AXIS))
    return jax.shard_map(
        functools.partial(on_device, n=mesh.shape[AXIS]),
        mesh=mesh,
        in_specs=in_specs,
        out_specs=out_specs,
        check_vma=False,
    )
```
